32 devices in a mesh: parts: 2 (over x), group: 4 (over y, core), local: 4 (over z).
Axes of the slice: x: 2, y: 2, z: 4, core: 2. Of those that a mesh axis runs over, the one named last changes fastest.
Arguments:
- x_quant: bfloat16 [4096, 3584], P(('parts', 'group', 'local')), parts along dimension 0, may hold values from -6 to 6
- row_scale: int32 [4096, 28], P(('parts', 'group', 'local')), parts along dimension 0, may hold values from -2 to 2
- grad_out: bfloat16 [4096, 3584], P(('parts', 'group', 'local')), parts along dimension 0, may hold values from -6 to 6
- expert_ids: int32 [4096, 1], P(('parts', 'group', 'local')), parts along dimension 0, may hold values from 0 to 3, as said below
- route_weight: float32 [4096, 1], P(('parts', 'group', 'local')), parts along dimension 0, may hold values from 0.1 to 0.6
- expert_gate_up: bfloat16 [4, 3584, 2, 1024], P('group', None, None, 'local'), may hold values from -0.09375 to 0.09375
- expert_down: bfloat16 [4, 1024, 3584], P('group', 'local'), may hold values from -0.1875 to 0.1875
Outputs:
- grad_tokens: bfloat16 [4096, 3584], P(('parts', 'group', 'local')), parts along dimension 0
- grad_expert_gate_up: bfloat16 [8, 3584, 2, 1024], P(('parts', 'group'), None, None, 'local'), parts along dimension 0
- grad_expert_down: bfloat16 [8, 1024, 3584], P(('parts', 'group'), 'local'), parts along dimension 0
The draws below stay inside these ranges and needn't reach their ends.
There are 2 independent parts, one for each index of `parts`. The reference program is written for one: setup_inputs(seed, part) draws one part's arguments, and reference() takes and returns one part's arrays. A program takes and returns all parts, laid end to end along the dimension named above; an argument that names none is the same for every part. Nothing has to cross between parts.
Inputs may be any that keep to these rules, and one draw needn't show every extreme that they name: `expert_ids`: each row names one expert, expert e lying in node group e. Among the 128 rows of one device no expert is named more than 40 times, some expert exactly 40 times, and every expert at least once.
All inputs are finite; a program needn't handle non-finite values.
Results may differ from the reference program's by a relative error of at most 0.007.
Values may be sent and summed in bfloat16 or wider, within the bound.
No kernel may reach another device: no remote copies, remote signals or barrier semaphores. Data moves between devices by JAX's collectives and lax.ppermute only.
A program may use at most 128 MiB of HBM per device.

```python
import jax
import jax.numpy as jnp
from jax import lax

D = 3584
FF = 1024
TOPK = 1
QB = 128
TOK_DEV = 128
EXPERTS = 4
TOKENS = 2048
MEAN = 32
CAP = 40
N_GROUP = 4
N_LOCAL = 4


def draw_expert_ids(key, part):
    key = jax.random.fold_in(key, 11)
    n_blocks = TOKENS // TOK_DEV
    extra = CAP - MEAN

    def block_ids(block_key):
        key_perm, key_amount, key_shuffle = jax.random.split(block_key, 3)
        labels = jax.random.permutation(key_perm, EXPERTS)
        amounts = jax.random.randint(key_amount, (EXPERTS // 2,), 0, extra + 1)
        amounts = amounts.at[0].set(extra)
        loads = jnp.stack([MEAN + amounts, MEAN - amounts], axis=1).reshape(-1)
        bounds = jnp.cumsum(loads)
        position = jnp.arange(TOPK * TOK_DEV)
        ranking = jnp.sum((position[:, None] >= bounds[None, :]).astype(jnp.int32), axis=1)
        listing = labels[ranking]
        shuffle = jax.random.permutation(key_shuffle, TOK_DEV)
        columns = [listing[shuffle + slot * TOK_DEV] for slot in range(TOPK)]
        return jnp.stack(columns, axis=1)
    block_keys = jax.random.split(key, n_blocks)
    return jax.vmap(block_ids)(block_keys).reshape(TOKENS, TOPK).astype(jnp.int32)


def touch_ends(drawn, rng, low, largest):
    longest = drawn.shape.index(max(drawn.shape))
    spots = []
    for shift in (0, 1):
        where = [jax.random.randint(jax.random.fold_in(rng, axis), (), 0, length) for axis, length in enumerate(drawn.shape)]
        where[longest] = (where[longest] + shift) % drawn.shape[longest]
        spots.append(tuple(where))
    return drawn.at[spots[0]].set(low).at[spots[1]].set(largest)


def block_scale(rng, dims, pieces, low, high):
    def one(dim, blocks):
        steps = jax.random.uniform(jax.random.fold_in(jax.random.fold_in(rng, 6), dim), (blocks,), jnp.float32, low / len(pieces), high / len(pieces))
        return jnp.repeat(jnp.exp(steps), dims[dim] // blocks).reshape((-1,) + (1,) * (len(dims) - dim - 1))

    factor_of = one(*pieces[0])
    for cut in pieces[1:]:
        factor_of = factor_of * one(*cut)
    return factor_of


def noise(key, shape, spread, reach, shards=(), held_as=jnp.bfloat16):
    entries = jax.random.normal(key, shape, jnp.float32) * spread
    if len(shards) > 0:
        entries = block_scale(key, shape, shards, -0.22, 0.18) * entries
    return jnp.clip(entries, min=-reach, max=reach).astype(held_as)


def setup_inputs(seed: int = 0, part: int = 0) -> dict:
    seeds = jax.random.split(jax.random.key(seed), 8)
    part_keys = jax.random.split(jax.random.fold_in(seeds[7], part), 8)
    x_quant = noise(part_keys[0], (TOKENS, D), 1.0, 6.0, ((0, 16),))
    row_scale = touch_ends(jax.random.randint(part_keys[1], (TOKENS, D // QB), -2, 3), jax.random.fold_in(part_keys[1], 1), -2, 2).astype(jnp.int32)
    grad_out = noise(part_keys[2], (TOKENS, D), 1.0, 6.0, ((0, 16),))
    expert_ids = draw_expert_ids(jax.random.fold_in(jax.random.fold_in(seeds[7], part), 71), part)
    route_weight = jnp.clip(0.1 + 0.5 * jax.random.uniform(part_keys[4], (TOKENS, TOPK), jnp.float32) ** block_scale(part_keys[4], (TOKENS, TOPK), ((0, 16),), -0.2, 0.2), 0.1, 0.6)
    expert_gate_up = noise(seeds[5], (EXPERTS, D, 2, FF), D ** -0.5, 0.09375, ((0, 4), (3, 4)))
    expert_down = noise(seeds[6], (EXPERTS, FF, D), FF ** -0.5, 0.1875, ((0, 4), (1, 4)))
    return dict(x_quant=x_quant, row_scale=row_scale, grad_out=grad_out, expert_ids=expert_ids, route_weight=route_weight, expert_gate_up=expert_gate_up, expert_down=expert_down)


def dequant(x_quant, row_scale):
    tok_count, feat_width = x_quant.shape
    blocked = x_quant.astype(jnp.float32).reshape(tok_count, feat_width // QB, QB)
    blocked = blocked * jnp.exp2(row_scale.astype(jnp.float32))[:, :, None]
    return blocked.reshape(tok_count, feat_width).astype(jnp.bfloat16)


def expert_grads(in_rows, out_grad, gate_up_w, down_w):
    feat_width, two, slice_width = gate_up_w.shape
    joined_w = gate_up_w.reshape(feat_width, two * slice_width)
    both_act = jnp.dot(in_rows, joined_w, preferred_element_type=jnp.float32)
    gate_act = both_act[:, :slice_width]
    up_act = both_act[:, slice_width:]
    sig_gate = jax.nn.sigmoid(gate_act)
    silu_gate = gate_act * sig_gate
    hidden = (silu_gate * up_act).astype(jnp.bfloat16)
    hid_grad = lax.dot_general(out_grad, down_w, (((1,), (1,)), ((), ())), preferred_element_type=jnp.float32)
    gate_grad = (hid_grad * up_act * sig_gate * (1.0 + gate_act * (1.0 - sig_gate))).astype(jnp.bfloat16)
    up_grad = (hid_grad * silu_gate).astype(jnp.bfloat16)
    both_grad = jnp.concatenate([gate_grad, up_grad], axis=1)
    row_grad = lax.dot_general(both_grad, joined_w, (((1,), (1,)), ((), ())), preferred_element_type=jnp.float32)
    weight_grad = lax.dot_general(in_rows, both_grad, (((0,), (0,)), ((), ())), preferred_element_type=jnp.float32)
    down_weight_grad = lax.dot_general(hidden, out_grad, (((0,), (0,)), ((), ())), preferred_element_type=jnp.float32)
    return row_grad, weight_grad.reshape(feat_width, two, slice_width), down_weight_grad


def reference(x_quant, row_scale, grad_out, expert_ids, route_weight, expert_gate_up, expert_down):
    token_rows = dequant(x_quant, row_scale)
    flat_ids = expert_ids.reshape(-1)
    flat_weight = route_weight.reshape(-1)
    room_rows = N_GROUP * N_LOCAL * CAP
    slice_width = FF // N_LOCAL

    def expert_step(accumulated, expert_id):
        is_expert = flat_ids == expert_id
        picked = jnp.nonzero(is_expert, size=room_rows, fill_value=0)[0].astype(jnp.int32)
        valid_row = jnp.arange(room_rows, dtype=jnp.int32) < jnp.sum(is_expert.astype(jnp.int32))
        tok_index = picked // TOPK
        expert_rows = jnp.where(valid_row[:, None], token_rows[tok_index], jnp.zeros((), jnp.bfloat16))
        weight_sel = jnp.where(valid_row, flat_weight[picked], jnp.zeros((), flat_weight.dtype))
        scaled_grad = (weight_sel[:, None] * grad_out[tok_index].astype(jnp.float32)).astype(jnp.bfloat16)
        gate_up = expert_gate_up[expert_id]
        down_full = expert_down[expert_id]
        row_total = jnp.zeros((room_rows, D), jnp.float32)
        gu_parts = []
        down_parts = []
        for shard in range(N_LOCAL):
            low = shard * slice_width
            high = low + slice_width
            row_part, gu_part, down_part = expert_grads(expert_rows, scaled_grad, gate_up[:, :, low:high], down_full[low:high, :])
            row_total = row_total + lax.optimization_barrier(row_part.astype(jnp.bfloat16)).astype(jnp.float32)
            gu_parts.append(gu_part)
            down_parts.append(down_part)
        rounded = lax.optimization_barrier(row_total.astype(jnp.bfloat16)).astype(jnp.float32)
        rounded = jnp.where(valid_row[:, None], rounded, jnp.zeros((), jnp.float32))
        accumulated = accumulated.at[tok_index].add(rounded)
        gu_grad = jnp.concatenate(gu_parts, axis=2)
        dn_grad = jnp.concatenate(down_parts, axis=0)
        return accumulated, (gu_grad.astype(jnp.bfloat16), dn_grad.astype(jnp.bfloat16))

    start = jnp.zeros((TOKENS, D), jnp.float32)
    routed, stacked = lax.scan(expert_step, start, jnp.arange(EXPERTS, dtype=jnp.int32))
    return routed.astype(jnp.bfloat16), stacked[0], stacked[1]
```

```python
import jax
import jax.numpy as jnp
from jax import lax
from jax.sharding import PartitionSpec as P

TOPK = 1
QB = 128


def dequant(x_quant, row_scale):
    tok_count, feat_width = x_quant.shape
    blocked = x_quant.astype(jnp.float32).reshape(tok_count, feat_width // QB, QB)
    blocked = blocked * jnp.exp2(row_scale.astype(jnp.float32))[:, :, None]
    return blocked.reshape(tok_count, feat_width).astype(jnp.bfloat16)


def dot32(a, b, ca, cb):
    return lax.dot_general(a, b, (((ca,), (cb,)), ((), ())), preferred_element_type=jnp.float32)


def add32(*parts):
    total = parts[0].astype(jnp.float32)
    for part in parts[1:]:
        total = total + part.astype(jnp.float32)
    return total.astype(jnp.bfloat16)


def ordered(values, after):
    if not after:
        return values
    return lax.optimization_barrier((tuple(values), tuple(after)))[0]


def per_device(x_quant, row_scale, grad_out, expert_ids, route_weight, expert_gate_up, expert_down):
    token_rows = dequant(x_quant, row_scale)
    tok_dev, feat_width = x_quant.shape
    n_groups = lax.axis_size("group")
    n_locals = lax.axis_size("local")
    my_group = lax.axis_index("group")
    mean_load = TOPK * tok_dev // n_groups
    slot_cap = mean_load + mean_load // 4
    rel_ids = expert_ids.reshape(-1) ^ my_group
    one_hot = (rel_ids[:, None] == jnp.arange(n_groups, dtype=jnp.int32)[None, :]).astype(jnp.int32)
    earlier = jnp.cumsum(one_hot, axis=0) - one_hot
    slot_pos = jnp.sum(earlier * one_hot, axis=1)
    target = rel_ids * slot_cap + slot_pos
    pick = target[None, :] == jnp.arange(n_groups * slot_cap, dtype=jnp.int32)[:, None]
    pick = pick.astype(jnp.bfloat16)
    scaled = (route_weight * grad_out.astype(jnp.float32)).astype(jnp.bfloat16)
    send_rows = dot32(pick, token_rows, 1, 0).astype(jnp.bfloat16)
    send_grads = dot32(pick, scaled, 1, 0).astype(jnp.bfloat16)
    send = jnp.stack(
        [
            send_rows.reshape(n_groups, slot_cap, feat_width),
            send_grads.reshape(n_groups, slot_cap, feat_width),
        ],
        axis=1,
    )
    gate_up_w = expert_gate_up[0].reshape(feat_width, -1)
    down_w = expert_down[0]
    width = down_w.shape[0]

    def swap(v, j):
        return lax.ppermute(v, "group", [(i, i ^ j) for i in range(n_groups)])

    n_chunks = min(4, n_groups)
    per_chunk = n_groups // n_chunks
    order = [0, 2, 3, 1] if n_chunks == 4 else list(range(n_chunks))
    came = {}
    for c in order:
        for j in range(c * per_chunk, (c + 1) * per_chunk):
            came[j] = send[j] if j == 0 else swap(send[j], j)
    me = lax.axis_index("local")
    chunks = list(order)
    hops = n_locals - 1
    gather_queue = []
    for first in range(0, n_chunks, 2):
        pair = chunks[first : first + 2]
        gather_queue += [(c, k) for k in range(1, n_locals) for c in pair]
    own, ups, downs, kept, slots, ran = {}, {}, {}, {}, {}, {}
    reduce_up, reduce_down, summed = {}, {}, {}

    def compute(c):
        ring = [own[c]] + [
            jnp.where(me >= k, ups[c, k], downs[c, n_locals - k]) for k in range(1, n_locals)
        ]
        in_rows = jnp.concatenate([v[0] for v in ring], axis=0)
        out_grad = jnp.concatenate([v[1] for v in ring], axis=0)
        both_act = dot32(in_rows, gate_up_w, 1, 0)
        gate_act, up_act = both_act[:, :width], both_act[:, width:]
        sig_gate = jax.nn.sigmoid(gate_act)
        silu_gate = gate_act * sig_gate
        hidden = (silu_gate * up_act).astype(jnp.bfloat16)
        hid_grad = dot32(out_grad, down_w, 1, 1)
        gate_grad = hid_grad * up_act * sig_gate * (1.0 + gate_act * (1.0 - sig_gate))
        up_grad = hid_grad * silu_gate
        both_grad = jnp.concatenate([gate_grad, up_grad], axis=1).astype(jnp.bfloat16)
        row_grad = dot32(both_grad, gate_up_w, 1, 1).astype(jnp.bfloat16)
        kept[c] = (in_rows, out_grad, both_grad, hidden)
        slots[c] = row_grad.reshape(n_locals, per_chunk * slot_cap, feat_width)

    round_no = 0
    gathered = 0
    outputs = {}
    reduce_left = [(c, h) for c in chunks for h in range(1, n_locals)]
    while gathered < len(gather_queue) or reduce_left:
        inputs, tasks = [], []
        if gathered < len(gather_queue):
            c, k = gather_queue[gathered]
            gathered += 1
            if k == 1:
                parts = [came[j] for j in range(c * per_chunk, (c + 1) * per_chunk)]
                own[c] = jnp.stack(parts, axis=1).reshape(2, per_chunk * slot_cap, feat_width)
                inputs += [own[c], own[c]]
            else:
                inputs += [ups[c, k - 1], downs[c, k - 1]]
            tasks.append(("gather", c, k))
            lag, most = 2, 1
        else:
            lag, most = 1, 1
        taken = []
        for c, h in reduce_left:
            if len(taken) == most or any(c == d for d, _ in taken):
                continue
            before = ran.get((c, h - 1) if h > 1 else (c, "gather"))
            if before is None or before > round_no - lag:
                continue
            taken.append((c, h))
        for c, h in taken:
            reduce_left.remove((c, h))
            if h == 1:
                compute(c)
            up_part, down_part = slots[c][h], slots[c][n_locals - h]
            if h > 1:
                up_part = add32(up_part, reduce_up[c])
                down_part = add32(down_part, reduce_down[c])
            inputs += [up_part, down_part]
            tasks.append(("reduce", c, h))
            ran[c, h] = round_no
        inputs = ordered(inputs, outputs.get(round_no - 2, []))
        made = []
        for (kind, c, k), up, down in zip(tasks, inputs[::2], inputs[1::2]):
            if kind == "gather":
                pairs = [(i, i + 1) for i in range(k - 1, hops)]
                ups[c, k] = up = lax.ppermute(up, "local", pairs)
                pairs = [(i, i - 1) for i in range(n_locals - k, 0, -1)]
                downs[c, k] = down = lax.ppermute(down, "local", pairs)
                if k == hops:
                    ran[c, "gather"] = round_no
            else:
                pairs = [(i, i + 1) for i in range(0, k)]
                reduce_up[c] = up = lax.ppermute(up, "local", pairs)
                pairs = [(i, i - 1) for i in range(hops, hops - k, -1)]
                reduce_down[c] = down = lax.ppermute(down, "local", pairs)
                if k == hops:
                    summed[c] = add32(slots[c][0], up, down)
            made += [up, down]
        outputs[round_no] = made
        round_no += 1
    returned = {}
    for c in chunks:
        rows = summed[c].reshape(per_chunk, slot_cap, feat_width)
        for i in range(per_chunk):
            j = c * per_chunk + i
            returned[j] = rows[i] if j == 0 else swap(rows[i], j)
    all_rows, all_grads, all_both, all_hidden = zip(*(kept[c] for c in chunks))
    gate_up_grad = dot32(jnp.concatenate(all_rows), jnp.concatenate(all_both), 0, 0)
    down_grad = dot32(jnp.concatenate(all_hidden), jnp.concatenate(all_grads), 0, 0)
    back = jnp.concatenate([returned[j] for j in range(n_groups)], axis=0)
    routed = dot32(pick, back, 0, 0)
    return (
        routed.astype(jnp.bfloat16),
        gate_up_grad.astype(jnp.bfloat16).reshape(expert_gate_up.shape),
        down_grad.astype(jnp.bfloat16)[None],
    )


def solution(mesh):
    placed = (
        P(("parts", "group", "local"), None),
        P(("parts", "group", "local"), None),
        P(("parts", "group", "local"), None),
        P(("parts", "group", "local"), None),
        P(("parts", "group", "local"), None),
        P("group", None, None, "local"),
        P("group", "local", None),
    )
    return jax.shard_map(
        per_device,
        mesh=mesh,
        in_specs=placed,
        out_specs=(
            P(("parts", "group", "local"), None),
            P(("parts", "group"), None, None, "local"),
            P(("parts", "group"), "local", None),
        ),
        check_vma=False,
    )
```

```python
import jax
import jax.numpy as jnp
from jax import lax
from jax.sharding import PartitionSpec as P

TOPK = 1
QB = 128


def dequant(x_quant, row_scale):
    tok_count, feat_width = x_quant.shape
    blocked = x_quant.astype(jnp.float32).reshape(tok_count, feat_width // QB, QB)
    blocked = blocked * jnp.exp2(row_scale.astype(jnp.float32))[:, :, None]
    return blocked.reshape(tok_count, feat_width).astype(jnp.bfloat16)


def dot32(a, b, ca, cb):
    return lax.dot_general(a, b, (((ca,), (cb,)), ((), ())), preferred_element_type=jnp.float32)


def add32(*parts):
    total = parts[0].astype(jnp.float32)
    for part in parts[1:]:
        total = total + part.astype(jnp.float32)
    return total.astype(jnp.bfloat16)


def tie(value, after):
    return lax.optimization_barrier((value, tuple(after)))[0] if after else value


def legs(n):
    out = []
    half = 1
    while half < n:
        for step in range(half):
            pairs = []
            for base in range(0, n, 2 * half):
                left, right = base + half - 1, base + half
                if step == 0:
                    pairs += [(left, right), (right, left)]
                else:
                    pairs += [(left - step + 1, left - step), (right + step - 1, right + step)]
            out.append((half, step, pairs))
        half *= 2
    return out


class Gather:
    def __init__(self, own, n):
        self.held = own[None]
        self.legs = legs(n)
        self.arrived = []
        self.moving = None

    def take(self, i, after=()):
        half, step, pairs = self.legs[i]
        if step == 0:
            self.settle()
            self.moving = self.held
        self.moving = lax.ppermute(tie(self.moving, after), "local", pairs)
        self.arrived.append(self.moving)
        return self.moving

    def settle(self):
        if self.arrived:
            total = self.arrived[0]
            for more in self.arrived[1:]:
                total = total + more
            self.held = jnp.concatenate([self.held, total], axis=0)
            self.arrived = []

    def result(self):
        self.settle()
        return self.held


class Reduce:
    def __init__(self, shares, n):
        self.shares = shares
        self.legs = legs(n)[::-1]
        self.coming = None

    def take(self, i, after=()):
        half, step, pairs = self.legs[i]
        if self.shares.shape[0] == 2 * half:
            self.near, self.shares = self.shares[:half], self.shares[half:]
        out = self.shares if self.coming is None else add32(self.shares, self.coming)
        self.coming = lax.ppermute(tie(out, after), "local", [(b, a) for a, b in pairs])
        if step == 0:
            self.shares = add32(self.near, self.coming)
            self.coming = None
            return self.shares
        return self.coming


SWAPS = (0, 1, 2, 3)
ORDER = (0, 2, 3, 1)
GROUPS = ((0, 1), (2,), (3,))
TIES = {
    ("swap", 3): [("swap", 2)],
    ("g", 2, 0): [("g", 0, 0)],
    ("g", 3, 0): [("g", 1, 0), ("g", 0, 1)],
    ("g", 1, 1): [("g", 0, 1)],
    ("g", 2, 1): [("g", 1, 1)],
    ("g", 3, 1): [("g", 2, 1)],
    ("g", 2, 2): [("g", 0, 2)],
    ("g", 3, 2): [("g", 1, 2)],
    ("c", 2, 0): [("r", 0, 0)],
    ("r", 0, 1): [("g", 3, 1)],
    ("r", 0, 2): [("r", 2, 0)],
    ("r", 1, 0): [("r", 0, 0)],
    ("r", 1, 1): [("r", 0, 1)],
    ("r", 1, 2): [("r", 2, 1)],
    "wgu": [("r", 2, 0)],
    "wdn": [("r", 2, 1)],
}


def steps(n):
    todo = [("g", c, leg) for leg in range(n - 1) for c in range(4)]
    todo += [("c", c, 0) for c in range(len(GROUPS))] + [("w", 0, 0)]
    todo += [("r", c, leg) for c in range(len(GROUPS)) for leg in range(n - 1)]
    needs = {}
    for kind, c, leg in todo:
        need = [w for w in TIES.get((kind, c, leg), ()) if w in todo]
        if kind in "gr" and leg:
            need.append((kind, c, leg - 1))
        if kind == "c":
            need += [("g", i, n - 2) for i in GROUPS[c]]
        if kind == "r":
            need.append(("c", c, 0))
        if kind == "w":
            need += [("c", i, 0) for i in range(len(GROUPS) - 1)]
        needs[kind, c, leg] = need
    out = []
    while todo:
        ready = [t for t in todo if not any(w in todo for w in needs[t])]
        out.append(ready[0])
        todo.remove(ready[0])
    return out


def per_device(x_quant, row_scale, grad_out, expert_ids, route_weight, expert_gate_up, expert_down):
    token_rows = dequant(x_quant, row_scale)
    tok_dev, feat_width = x_quant.shape
    n_groups = lax.axis_size("group")
    n_locals = lax.axis_size("local")
    my_group = lax.axis_index("group")
    mean_load = TOPK * tok_dev // n_groups
    slot_cap = mean_load + mean_load // 4
    rel_ids = expert_ids.reshape(-1) ^ my_group
    one_hot = (rel_ids[:, None] == jnp.arange(n_groups, dtype=jnp.int32)[None, :]).astype(jnp.int32)
    earlier = jnp.cumsum(one_hot, axis=0) - one_hot
    slot_pos = jnp.sum(earlier * one_hot, axis=1)
    target = rel_ids * slot_cap + slot_pos
    pick = target[None, :] == jnp.arange(n_groups * slot_cap, dtype=jnp.int32)[:, None]
    pick = pick.astype(jnp.bfloat16)
    scaled = (route_weight * grad_out.astype(jnp.float32)).astype(jnp.bfloat16)
    send_rows = dot32(pick, token_rows, 1, 0).astype(jnp.bfloat16)
    send_grads = dot32(pick, scaled, 1, 0).astype(jnp.bfloat16)
    send = jnp.stack(
        [
            send_rows.reshape(n_groups, slot_cap, feat_width),
            send_grads.reshape(n_groups, slot_cap, feat_width),
        ],
        axis=1,
    )
    gate_up_w = expert_gate_up[0].reshape(feat_width, -1)
    down_w = expert_down[0]
    width = down_w.shape[0]

    def swap(v, j):
        return lax.ppermute(v, "group", [(i, i ^ j) for i in range(n_groups)])

    per_part = n_groups // 4
    parts = [list(range(p * per_part, (p + 1) * per_part)) for p in range(4)]
    part_rows = per_part * slot_cap
    order = ORDER
    done = {}

    def after(name):
        return [done[w] for w in TIES.get(name, ()) if w in done]

    def chunk_of(p):
        name = ("swap", p)
        came = [send[j] if j == 0 else swap(tie(send[j], after(name)), j) for j in parts[p]]
        return jnp.stack(came, axis=1).reshape(2, part_rows, feat_width)

    kept = {}

    def compute(c, held):
        in_rows = held[:, 0].reshape(-1, feat_width)
        out_grad = held[:, 1].reshape(-1, feat_width)
        both_act = dot32(in_rows, gate_up_w, 1, 0)
        gate_act, up_act = both_act[:, :width], both_act[:, width:]
        sig_gate = jax.nn.sigmoid(gate_act)
        silu_gate = gate_act * sig_gate
        hidden = (silu_gate * up_act).astype(jnp.bfloat16)
        hid_grad = dot32(out_grad, down_w, 1, 1)
        gate_grad = hid_grad * up_act * sig_gate * (1.0 + gate_act * (1.0 - sig_gate))
        up_grad = hid_grad * silu_gate
        both_grad = jnp.concatenate([gate_grad, up_grad], axis=1).astype(jnp.bfloat16)
        row_grad = dot32(both_grad, gate_up_w, 1, 1).astype(jnp.bfloat16)
        kept[c] = (in_rows, out_grad, both_grad, hidden)
        return row_grad.reshape(n_locals, -1, feat_width)

    def weight_grads(names):
        in_rows, out_grad, both_grad, hidden = (
            jnp.concatenate(v) for v in zip(*(kept[c] for c in names))
        )
        return dot32(in_rows, both_grad, 0, 0), dot32(hidden, out_grad, 0, 0)

    legs_no = n_locals - 1
    chunk = {}
    for p in SWAPS:
        done["swap", p] = chunk[p] = chunk_of(p)
    gathers = {p: Gather(chunk[p], n_locals) for p in order}
    reduces, shares = {}, {}

    def step(kind, c, leg):
        name = (kind, c, leg)
        if kind == "g":
            done[name] = gathers[order[c]].take(leg, after(name))
        elif kind == "c":
            held = [gathers[order[i]].result() for i in GROUPS[c]]
            held = held[0] if len(held) == 1 else jnp.concatenate(held, axis=2)
            shares[c] = compute(c, tie(held, after(name)))
            done[name] = shares[c]
            reduces[c] = Reduce(shares[c], n_locals)
        elif kind == "w":
            done[name] = partial = weight_grads(range(len(GROUPS) - 1))
            partials.append(partial)
        else:
            done[name] = reduces[c].take(leg, after(name))

    partials = []
    for name in steps(n_locals):
        step(*name)
    final = len(GROUPS) - 1
    held_gu, held_down = partials[0]
    last_gu, last_down = weight_grads([final])
    gate_up_grad = tie(held_gu, after("wgu")) + last_gu
    down_grad = tie(held_down, after("wdn")) + last_down
    returned = {}
    for c, members in enumerate(GROUPS):
        rows = tie(done["r", c, legs_no - 1], after(("back", c)))
        rows = rows.reshape(len(members), per_part, slot_cap, feat_width)
        for m, i in enumerate(members):
            for q, j in enumerate(parts[order[i]]):
                returned[j] = rows[m, q] if j == 0 else swap(rows[m, q], j)
    back = jnp.concatenate([returned[j] for j in range(n_groups)], axis=0)
    routed = dot32(pick, back, 0, 0)
    return (
        routed.astype(jnp.bfloat16),
        gate_up_grad.astype(jnp.bfloat16).reshape(expert_gate_up.shape),
        down_grad.astype(jnp.bfloat16)[None],
    )


def solution(mesh):
    placed = (
        P(("parts", "group", "local"), None),
        P(("parts", "group", "local"), None),
        P(("parts", "group", "local"), None),
        P(("parts", "group", "local"), None),
        P(("parts", "group", "local"), None),
        P("group", None, None, "local"),
        P("group", "local", None),
    )
    return jax.shard_map(
        per_device,
        mesh=mesh,
        in_specs=placed,
        out_specs=(
            P(("parts", "group", "local"), None),
            P(("parts", "group"), None, None, "local"),
            P(("parts", "group"), "local", None),
        ),
        check_vma=False,
    )
```

```python
import jax
import jax.numpy as jnp
from jax import lax
from jax.sharding import PartitionSpec as P

TOPK = 1
QB = 128


def dequant(x_quant, row_scale):
    tok_count, feat_width = x_quant.shape
    blocked = x_quant.astype(jnp.float32).reshape(tok_count, feat_width // QB, QB)
    blocked = blocked * jnp.exp2(row_scale.astype(jnp.float32))[:, :, None]
    return blocked.reshape(tok_count, feat_width).astype(jnp.bfloat16)


def dot32(a, b, ca, cb):
    return lax.dot_general(a, b, (((ca,), (cb,)), ((), ())), preferred_element_type=jnp.float32)


def add32(*parts):
    total = parts[0].astype(jnp.float32)
    for part in parts[1:]:
        total = total + part.astype(jnp.float32)
    return total.astype(jnp.bfloat16)


def tie(value, after):
    return lax.optimization_barrier((value, tuple(after)))[0] if after else value


def legs(n):
    out = []
    half = 1
    while half < n:
        for step in range(half):
            pairs = []
            for base in range(0, n, 2 * half):
                left, right = base + half - 1, base + half
                if step == 0:
                    pairs += [(left, right), (right, left)]
                else:
                    pairs += [(left - step + 1, left - step), (right + step - 1, right + step)]
            out.append((half, step, pairs))
        half *= 2
    return out


def held_blocks(n):
    held = [[z] for z in range(n)]
    moving = None
    for half, step, pairs in legs(n):
        if step == 0:
            moving = [list(h) for h in held]
            grown = [None] * n
        before = [list(m) for m in moving]
        for a, b in pairs:
            moving[b] = before[a]
            grown[b] = held[b] + before[a]
        if step == half - 1:
            held = grown
    return held


class Gather:
    def __init__(self, own, n, direct):
        self.held = own[None]
        self.n = n
        self.direct = direct
        self.arrived = []
        self.moving = None

    def take(self, i, after=()):
        if self.direct:
            own = tie(self.held, after)
            for k in range(1, self.n):
                pairs = [(z, z ^ k) for z in range(self.n)]
                self.arrived.append(lax.ppermute(own, "local", pairs))
            return self.arrived
        half, step, pairs = legs(self.n)[i]
        if step == 0:
            self.settle()
            self.moving = self.held
        self.moving = lax.ppermute(tie(self.moving, after), "local", pairs)
        self.arrived.append(self.moving)
        return [self.moving]

    def settle(self):
        if self.arrived and self.direct:
            self.held = jnp.concatenate([self.held] + self.arrived, axis=0)
        elif self.arrived:
            total = self.arrived[0]
            for more in self.arrived[1:]:
                total = total + more
            self.held = jnp.concatenate([self.held, total], axis=0)
        self.arrived = []

    def result(self):
        self.settle()
        return self.held


class Reduce:
    def __init__(self, shares, n, direct, direct_order=False):
        self.n = n
        self.direct = direct
        if direct and not direct_order:
            held = held_blocks(n)
            me = lax.axis_index("local")
            pick = [[held[z].index(z ^ k) for z in range(n)] for k in range(n)]
            spots = [jnp.asarray(places, jnp.int32)[me] for places in pick]
            shares = [lax.dynamic_index_in_dim(shares, at, 0, keepdims=False) for at in spots]
        self.shares = shares
        self.coming = None

    def take(self, i, after=()):
        if self.direct:
            shares = tie(tuple(self.shares), after)
            came = {}
            for k in [k for k in FAR_FIRST if k < self.n] + list(range(4, self.n)):
                pairs = [(z, z ^ k) for z in range(self.n)]
                came[k] = lax.ppermute(shares[k], "local", pairs)
            came = list(came.values())
            self.shares = add32(shares[0], *came)[None]
            return came
        half, step, pairs = legs(self.n)[::-1][i]
        if self.shares.shape[0] == 2 * half:
            self.near, self.shares = self.shares[:half], self.shares[half:]
        out = self.shares if self.coming is None else add32(self.shares, self.coming)
        came = lax.ppermute(tie(out, after), "local", [(b, a) for a, b in pairs])
        self.coming = came
        if step == 0:
            self.shares = add32(self.near, came)
            self.coming = None
        return [came]


FAR_FIRST = (3, 2, 1)
CHUNKS = (((0, 0, 5),), ((2, 0, 5),), ((3, 0, 5),), ((1, 0, 5),))
JOINED = {}
GROUPS = ((0,), (1,), (2,), (3,))
DIRECT_GATHERS = ()
DIRECT_REDUCES = ()
RANK = {}
TIES = {
    ('g', 2, 0): [('g', 0, 0)],
    ('g', 3, 0): [('g', 1, 0)],
    ('g', 0, 1): [('s', 2, 0)],
    ('g', 1, 1): [('g', 0, 1), ('g', 2, 0), ('s', 3, 0)],
    ('g', 2, 1): [('g', 1, 1)],
    ('g', 3, 1): [('g', 2, 1)],
    ('g', 0, 2): [('g', 3, 0)],
    ('g', 2, 2): [('g', 0, 2)],
    ('g', 3, 2): [('g', 1, 2)],
    ('c', 3, 0): [('r', 1, 0)],
    ('r', 0, 1): [('g', 3, 1)],
    ('r', 0, 2): [('r', 3, 0)],
    ('r', 1, 1): [('r', 0, 1)],
    ('r', 1, 2): [('r', 3, 0)],
    ('r', 2, 1): [('r', 1, 1)],
    ('r', 2, 2): [('r', 3, 0)],
    ('v', 0, 0): [('r', 3, 0)],
    ('r', 3, 2): [('v', 0, 0)],
    ('r', 3, 1): [('v', 1, 0)],
}


def steps(n):
    todo = [("s", p, 0) for p in range(4)]
    for p in range(len(CHUNKS)):
        todo += [("g", p, leg) for leg in range(1 if p in DIRECT_GATHERS else n - 1)]
    lead = {i: c for c, members in JOINED.items() for i in members}
    todo = [t for t in todo if t[0] != "g" or t[2] or lead.get(t[1], t[1]) == t[1]]
    todo += [("c", c, 0) for c in range(len(GROUPS))]
    todo += [("w", 0, 0), ("v", 0, 0), ("v", 1, 0)]
    for c in range(len(GROUPS)):
        todo += [("r", c, leg) for leg in range(1 if c in DIRECT_REDUCES else n - 1)]
    todo.sort(key=lambda t: RANK.get(t, 99))
    out = []
    while todo:
        for t in todo:
            kind, c, leg = t
            need = [w for w in TIES.get(t, ()) if w in todo]
            if kind == "g":
                if leg:
                    need.append(("g", lead.get(c, c) if leg == 1 else c, leg - 1))
                else:
                    need += [("s", p, 0) for i in JOINED.get(c, (c,)) for p, _, _ in CHUNKS[i]]
            elif kind == "c":
                need += [w for w in todo if w[0] == "g" and w[1] in GROUPS[c]]
            elif kind == "r":
                need.append(("r", c, leg - 1) if leg else ("c", c, 0))
            elif kind == "v":
                need += [("w", 0, 0), ("c", len(GROUPS) - 1, 0)]
            elif kind == "w":
                need += [("c", i, 0) for i in range(len(GROUPS) - 1)]
            if not any(w in todo for w in need):
                out.append(t)
                todo.remove(t)
                break
        else:
            raise ValueError("cyclic waits")
    return out


def per_device(x_quant, row_scale, grad_out, expert_ids, route_weight, expert_gate_up, expert_down):
    token_rows = dequant(x_quant, row_scale)
    tok_dev, feat_width = x_quant.shape
    n_groups = lax.axis_size("group")
    n_locals = lax.axis_size("local")
    my_group = lax.axis_index("group")
    mean_load = TOPK * tok_dev // n_groups
    slot_cap = mean_load + mean_load // 4
    rel_ids = expert_ids.reshape(-1) ^ my_group
    one_hot = (rel_ids[:, None] == jnp.arange(n_groups, dtype=jnp.int32)[None, :]).astype(jnp.int32)
    earlier = jnp.cumsum(one_hot, axis=0) - one_hot
    slot_pos = jnp.sum(earlier * one_hot, axis=1)
    target = rel_ids * slot_cap + slot_pos
    pick = target[None, :] == jnp.arange(n_groups * slot_cap, dtype=jnp.int32)[:, None]
    pick = pick.astype(jnp.bfloat16)
    scaled = (route_weight * grad_out.astype(jnp.float32)).astype(jnp.bfloat16)
    send_rows = dot32(pick, token_rows, 1, 0).astype(jnp.bfloat16)
    send_grads = dot32(pick, scaled, 1, 0).astype(jnp.bfloat16)
    send = jnp.stack(
        [
            send_rows.reshape(n_groups, slot_cap, feat_width),
            send_grads.reshape(n_groups, slot_cap, feat_width),
        ],
        axis=1,
    )
    gate_up_w = expert_gate_up[0].reshape(feat_width, -1)
    down_w = expert_down[0]
    width = down_w.shape[0]

    def swap(v, j):
        return lax.ppermute(v, "group", [(i, i ^ j) for i in range(n_groups)])

    per_part = n_groups // 4
    parts = [list(range(p * per_part, (p + 1) * per_part)) for p in range(4)]
    part_rows = per_part * slot_cap
    done = {}

    def cut(fifths):
        return part_rows * fifths // 5

    def after(name):
        return [v for w in TIES.get(name, ()) for v in done.get(w, ())]

    kept = {}

    def compute(c, held):
        in_rows = held[:, 0].reshape(-1, feat_width)
        out_grad = held[:, 1].reshape(-1, feat_width)
        both_act = dot32(in_rows, gate_up_w, 1, 0)
        gate_act, up_act = both_act[:, :width], both_act[:, width:]
        sig_gate = jax.nn.sigmoid(gate_act)
        silu_gate = gate_act * sig_gate
        hidden = (silu_gate * up_act).astype(jnp.bfloat16)
        hid_grad = dot32(out_grad, down_w, 1, 1)
        gate_grad = hid_grad * up_act * sig_gate * (1.0 + gate_act * (1.0 - sig_gate))
        up_grad = hid_grad * silu_gate
        both_grad = jnp.concatenate([gate_grad, up_grad], axis=1).astype(jnp.bfloat16)
        row_grad = dot32(both_grad, gate_up_w, 1, 1).astype(jnp.bfloat16)
        kept[c] = (in_rows, out_grad, both_grad, hidden)
        return row_grad.reshape(n_locals, -1, feat_width)

    def weight_grads(names):
        in_rows, out_grad, both_grad, hidden = (
            jnp.concatenate(v) for v in zip(*(kept[c] for c in names))
        )
        return dot32(in_rows, both_grad, 0, 0), dot32(hidden, out_grad, 0, 0)

    chunk, gathers, reduces, partial, whole = {}, {}, {}, [], [None, None]
    final = len(GROUPS) - 1
    for kind, c, leg in steps(n_locals):
        name = (kind, c, leg)
        waits = after(name)
        if kind == "s":
            came = [send[j] if j == 0 else swap(tie(send[j], waits), j) for j in parts[c]]
            chunk[c] = jnp.stack(came, axis=1).reshape(2, part_rows, feat_width)
            done[name] = [chunk[c]]
        elif kind == "g":
            if leg == 0:
                mine = {}
                for i in JOINED.get(c, (c,)):
                    pieces = [chunk[p][:, cut(lo) : cut(hi)] for p, lo, hi in CHUNKS[i]]
                    mine[i] = pieces[0] if len(pieces) == 1 else jnp.concatenate(pieces, axis=1)
                    gathers[i] = Gather(mine[i], n_locals, c in DIRECT_GATHERS)
                if len(mine) == 1:
                    done[name] = gathers[c].take(0, waits)
                else:
                    joint = Gather(jnp.concatenate(list(mine.values()), axis=1), n_locals, False)
                    done[name] = joint.take(0, waits)
                    at = 0
                    for i, rows in mine.items():
                        end = at + rows.shape[1]
                        gathers[i].arrived = [done[name][0][:, :, at:end]]
                        at = end
            else:
                done[name] = gathers[c].take(leg, waits)
        elif kind == "c":
            held = [gathers[p].result() for p in GROUPS[c]]
            held = held[0] if len(held) == 1 else jnp.concatenate(held, axis=2)
            shares = compute(c, tie(held, waits))
            done[name] = [shares]
            straight = GROUPS[c][0] in DIRECT_GATHERS
            reduces[c] = Reduce(shares, n_locals, c in DIRECT_REDUCES, straight)
        elif kind == "w":
            partial = weight_grads(range(final))
            done[name] = list(partial)
        elif kind == "v":
            rest = weight_grads([final])[c]
            total = (tie(partial[c], waits) + rest).astype(jnp.bfloat16)
            whole[c] = total.reshape(expert_gate_up.shape) if c == 0 else total[None]
            done[name] = [whole[c]]
        else:
            done[name] = reduces[c].take(leg, waits)
    gate_up_grad, down_grad = whole
    pieces = {p: [] for p in range(4)}
    for c, members in enumerate(GROUPS):
        rows = tie(reduces[c].shares, after(("b", c, 0)))[0]
        at = 0
        for p, lo, hi in [piece for member in members for piece in CHUNKS[member]]:
            size = cut(hi) - cut(lo)
            pieces[p].append((lo, rows[at : at + size]))
            at += size
    returned = {}
    for p in range(4):
        rows = [v for _, v in sorted(pieces[p], key=lambda piece: piece[0])]
        rows = rows[0] if len(rows) == 1 else jnp.concatenate(rows)
        rows = rows.reshape(per_part, slot_cap, feat_width)
        for q, j in enumerate(parts[p]):
            returned[j] = rows[q] if j == 0 else swap(rows[q], j)
    back = jnp.concatenate([returned[j] for j in range(n_groups)], axis=0)
    routed = dot32(pick, back, 0, 0)
    return (
        routed.astype(jnp.bfloat16),
        gate_up_grad,
        down_grad,
    )


def solution(mesh):
    placed = (
        P(("parts", "group", "local"), None),
        P(("parts", "group", "local"), None),
        P(("parts", "group", "local"), None),
        P(("parts", "group", "local"), None),
        P(("parts", "group", "local"), None),
        P("group", None, None, "local"),
        P("group", "local", None),
    )
    return jax.shard_map(
        per_device,
        mesh=mesh,
        in_specs=placed,
        out_specs=(
            P(("parts", "group", "local"), None),
            P(("parts", "group"), None, None, "local"),
            P(("parts", "group"), "local", None),
        ),
        check_vma=False,
    )
```

```python
import jax
import jax.numpy as jnp
from jax import lax
from jax.sharding import PartitionSpec as P

TOPK = 1
QB = 128


def dequant(x_quant, row_scale):
    tok_count, feat_width = x_quant.shape
    blocked = x_quant.astype(jnp.float32).reshape(tok_count, feat_width // QB, QB)
    blocked = blocked * jnp.exp2(row_scale.astype(jnp.float32))[:, :, None]
    return blocked.reshape(tok_count, feat_width).astype(jnp.bfloat16)


def dot32(a, b, ca, cb):
    return lax.dot_general(a, b, (((ca,), (cb,)), ((), ())), preferred_element_type=jnp.float32)


def add32(*parts):
    total = parts[0].astype(jnp.float32)
    for part in parts[1:]:
        total = total + part.astype(jnp.float32)
    return total.astype(jnp.bfloat16)


def tie(value, after):
    return lax.optimization_barrier((value, tuple(after)))[0] if after else value


def legs(n):
    out = []
    half = 1
    while half < n:
        for step in range(half):
            pairs = []
            for base in range(0, n, 2 * half):
                left, right = base + half - 1, base + half
                if step == 0:
                    pairs += [(left, right), (right, left)]
                else:
                    pairs += [(left - step + 1, left - step), (right + step - 1, right + step)]
            out.append((half, step, pairs))
        half *= 2
    return out


def held_blocks(n):
    held = [[z] for z in range(n)]
    moving = None
    for half, step, pairs in legs(n):
        if step == 0:
            moving = [list(h) for h in held]
            grown = [None] * n
        before = [list(m) for m in moving]
        for a, b in pairs:
            moving[b] = before[a]
            grown[b] = held[b] + before[a]
        if step == half - 1:
            held = grown
    return held


class Gather:
    def __init__(self, own, n, direct):
        self.held = own[None]
        self.n = n
        self.direct = direct
        self.arrived = []
        self.moving = None

    def take(self, i, after=()):
        if self.direct:
            own = tie(self.held, after)
            for k in range(1, self.n):
                pairs = [(z, z ^ k) for z in range(self.n)]
                self.arrived.append(lax.ppermute(own, "local", pairs))
            return self.arrived
        half, step, pairs = legs(self.n)[i]
        if step == 0:
            self.settle()
            self.moving = self.held
        self.moving = lax.ppermute(tie(self.moving, after), "local", pairs)
        self.arrived.append(self.moving)
        return [self.moving]

    def settle(self):
        if self.arrived and self.direct:
            self.held = jnp.concatenate([self.held] + self.arrived, axis=0)
        elif self.arrived:
            total = self.arrived[0]
            for more in self.arrived[1:]:
                total = total + more
            self.held = jnp.concatenate([self.held, total], axis=0)
        self.arrived = []

    def result(self):
        self.settle()
        return self.held


class Reduce:
    def __init__(self, shares, n, direct, direct_order=False):
        self.n = n
        self.direct = direct
        if direct and not direct_order:
            held = held_blocks(n)
            me = lax.axis_index("local")
            pick = [[held[z].index(z ^ k) for z in range(n)] for k in range(n)]
            spots = [jnp.asarray(places, jnp.int32)[me] for places in pick]
            shares = [lax.dynamic_index_in_dim(shares, at, 0, keepdims=False) for at in spots]
        self.shares = shares
        self.coming = None

    def take(self, i, after=()):
        if self.direct:
            shares = tie(tuple(self.shares), after)
            came = {}
            for k in [k for k in FAR_FIRST if k < self.n] + list(range(4, self.n)):
                pairs = [(z, z ^ k) for z in range(self.n)]
                came[k] = lax.ppermute(shares[k], "local", pairs)
            came = list(came.values())
            self.shares = add32(shares[0], *came)[None]
            return came
        half, step, pairs = legs(self.n)[::-1][i]
        if self.shares.shape[0] == 2 * half:
            self.near, self.shares = self.shares[:half], self.shares[half:]
        out = self.shares if self.coming is None else add32(self.shares, self.coming)
        came = lax.ppermute(tie(out, after), "local", [(b, a) for a, b in pairs])
        self.coming = came
        if step == 0:
            self.shares = add32(self.near, came)
            self.coming = None
        return [came]


FAR_FIRST = (3, 2, 1)
CHUNKS = (((0, 0, 5),), ((2, 0, 5),), ((3, 0, 5),), ((1, 0, 5),))
JOINED = {}
GROUPS = ((0,), (1,), (2,), (3,))
DIRECT_GATHERS = ()
DIRECT_REDUCES = ()
RANK = {}
TIES = {
    ('g', 2, 0): [('g', 0, 0)],
    ('g', 3, 0): [('g', 1, 0)],
    ('g', 0, 1): [('s', 2, 0)],
    ('g', 1, 1): [('g', 0, 1)],
    ('g', 2, 1): [('g', 1, 1), ('g', 2, 0)],
    ('g', 3, 1): [('g', 2, 1)],
    ('g', 0, 2): [('g', 3, 0), ('g', 0, 1)],
    ('g', 2, 2): [('g', 0, 2)],
    ('g', 3, 2): [('g', 1, 2)],
    ('c', 3, 0): [('r', 1, 0)],
    ('r', 0, 1): [('g', 3, 1)],
    ('r', 0, 2): [('r', 3, 0)],
    ('r', 1, 1): [('r', 0, 1)],
    ('r', 1, 2): [('r', 3, 0)],
    ('r', 2, 1): [('r', 1, 1)],
    ('r', 2, 2): [('r', 3, 0)],
    ('v', 0, 0): [('r', 3, 0)],
    ('r', 3, 2): [('v', 0, 0)],
    ('r', 3, 1): [('v', 1, 0)],
    ('g', 1, 2): [('g', 2, 0)],
    ('w', 0, 0): [('g', 3, 2)],
    ('v', 1, 0): [('r', 3, 0)],
    ('r', 0, 0): [('r', 1, 0)],
}


def steps(n):
    todo = [("s", p, 0) for p in range(4)]
    for p in range(len(CHUNKS)):
        todo += [("g", p, leg) for leg in range(1 if p in DIRECT_GATHERS else n - 1)]
    lead = {i: c for c, members in JOINED.items() for i in members}
    todo = [t for t in todo if t[0] != "g" or t[2] or lead.get(t[1], t[1]) == t[1]]
    todo += [("c", c, 0) for c in range(len(GROUPS))]
    todo += [("w", 0, 0), ("v", 0, 0), ("v", 1, 0)]
    for c in range(len(GROUPS)):
        todo += [("r", c, leg) for leg in range(1 if c in DIRECT_REDUCES else n - 1)]
    todo.sort(key=lambda t: RANK.get(t, 99))
    out = []
    while todo:
        for t in todo:
            kind, c, leg = t
            need = [w for w in TIES.get(t, ()) if w in todo]
            if kind == "g":
                if leg:
                    need.append(("g", lead.get(c, c) if leg == 1 else c, leg - 1))
                else:
                    need += [("s", p, 0) for i in JOINED.get(c, (c,)) for p, _, _ in CHUNKS[i]]
            elif kind == "c":
                need += [w for w in todo if w[0] == "g" and w[1] in GROUPS[c]]
            elif kind == "r":
                need.append(("r", c, leg - 1) if leg else ("c", c, 0))
            elif kind == "v":
                need += [("w", 0, 0), ("c", len(GROUPS) - 1, 0)]
            elif kind == "w":
                need += [("c", i, 0) for i in range(len(GROUPS) - 1)]
            if not any(w in todo for w in need):
                out.append(t)
                todo.remove(t)
                break
        else:
            raise ValueError("cyclic waits")
    return out


def per_device(x_quant, row_scale, grad_out, expert_ids, route_weight, expert_gate_up, expert_down):
    token_rows = dequant(x_quant, row_scale)
    tok_dev, feat_width = x_quant.shape
    n_groups = lax.axis_size("group")
    n_locals = lax.axis_size("local")
    my_group = lax.axis_index("group")
    mean_load = TOPK * tok_dev // n_groups
    slot_cap = mean_load + mean_load // 4
    rel_ids = expert_ids.reshape(-1) ^ my_group
    one_hot = (rel_ids[:, None] == jnp.arange(n_groups, dtype=jnp.int32)[None, :]).astype(jnp.int32)
    earlier = jnp.cumsum(one_hot, axis=0) - one_hot
    slot_pos = jnp.sum(earlier * one_hot, axis=1)
    target = rel_ids * slot_cap + slot_pos
    pick = target[None, :] == jnp.arange(n_groups * slot_cap, dtype=jnp.int32)[:, None]
    pick = pick.astype(jnp.bfloat16)
    scaled = (route_weight * grad_out.astype(jnp.float32)).astype(jnp.bfloat16)
    send_rows = dot32(pick, token_rows, 1, 0).astype(jnp.bfloat16)
    send_grads = dot32(pick, scaled, 1, 0).astype(jnp.bfloat16)
    send = jnp.stack(
        [
            send_rows.reshape(n_groups, slot_cap, feat_width),
            send_grads.reshape(n_groups, slot_cap, feat_width),
        ],
        axis=1,
    )
    gate_up_w = expert_gate_up[0].reshape(feat_width, -1)
    down_w = expert_down[0]
    width = down_w.shape[0]

    def swap(v, j):
        return lax.ppermute(v, "group", [(i, i ^ j) for i in range(n_groups)])

    per_part = n_groups // 4
    parts = [list(range(p * per_part, (p + 1) * per_part)) for p in range(4)]
    part_rows = per_part * slot_cap
    done = {}

    def cut(fifths):
        return part_rows * fifths // 5

    def after(name):
        return [v for w in TIES.get(name, ()) for v in done.get(w, ())]

    kept = {}

    def compute(c, held):
        in_rows = held[:, 0].reshape(-1, feat_width)
        out_grad = held[:, 1].reshape(-1, feat_width)
        both_act = dot32(in_rows, gate_up_w, 1, 0)
        gate_act, up_act = both_act[:, :width], both_act[:, width:]
        sig_gate = jax.nn.sigmoid(gate_act)
        silu_gate = gate_act * sig_gate
        hidden = (silu_gate * up_act).astype(jnp.bfloat16)
        hid_grad = dot32(out_grad, down_w, 1, 1)
        gate_grad = hid_grad * up_act * sig_gate * (1.0 + gate_act * (1.0 - sig_gate))
        up_grad = hid_grad * silu_gate
        both_grad = jnp.concatenate([gate_grad, up_grad], axis=1).astype(jnp.bfloat16)
        row_grad = dot32(both_grad, gate_up_w, 1, 1).astype(jnp.bfloat16)
        kept[c] = (in_rows, out_grad, both_grad, hidden)
        return row_grad.reshape(n_locals, -1, feat_width)

    def weight_grads(names):
        in_rows, out_grad, both_grad, hidden = (
            jnp.concatenate(v) for v in zip(*(kept[c] for c in names))
        )
        return dot32(in_rows, both_grad, 0, 0), dot32(hidden, out_grad, 0, 0)

    chunk, gathers, reduces, partial, whole = {}, {}, {}, [], [None, None]
    final = len(GROUPS) - 1
    for kind, c, leg in steps(n_locals):
        name = (kind, c, leg)
        waits = after(name)
        if kind == "s":
            came = [send[j] if j == 0 else swap(tie(send[j], waits), j) for j in parts[c]]
            chunk[c] = jnp.stack(came, axis=1).reshape(2, part_rows, feat_width)
            done[name] = [chunk[c]]
        elif kind == "g":
            if leg == 0:
                mine = {}
                for i in JOINED.get(c, (c,)):
                    pieces = [chunk[p][:, cut(lo) : cut(hi)] for p, lo, hi in CHUNKS[i]]
                    mine[i] = pieces[0] if len(pieces) == 1 else jnp.concatenate(pieces, axis=1)
                    gathers[i] = Gather(mine[i], n_locals, c in DIRECT_GATHERS)
                if len(mine) == 1:
                    done[name] = gathers[c].take(0, waits)
                else:
                    joint = Gather(jnp.concatenate(list(mine.values()), axis=1), n_locals, False)
                    done[name] = joint.take(0, waits)
                    at = 0
                    for i, rows in mine.items():
                        end = at + rows.shape[1]
                        gathers[i].arrived = [done[name][0][:, :, at:end]]
                        at = end
            else:
                done[name] = gathers[c].take(leg, waits)
        elif kind == "c":
            held = [gathers[p].result() for p in GROUPS[c]]
            held = held[0] if len(held) == 1 else jnp.concatenate(held, axis=2)
            shares = compute(c, tie(held, waits))
            done[name] = [shares]
            straight = GROUPS[c][0] in DIRECT_GATHERS
            reduces[c] = Reduce(shares, n_locals, c in DIRECT_REDUCES, straight)
        elif kind == "w":
            partial = weight_grads(range(final))
            done[name] = list(partial)
        elif kind == "v":
            rest = weight_grads([final])[c]
            total = (tie(partial[c], waits) + rest).astype(jnp.bfloat16)
            whole[c] = total.reshape(expert_gate_up.shape) if c == 0 else total[None]
            done[name] = [whole[c]]
        else:
            done[name] = reduces[c].take(leg, waits)
    gate_up_grad, down_grad = whole
    pieces = {p: [] for p in range(4)}
    for c, members in enumerate(GROUPS):
        rows = tie(reduces[c].shares, after(("b", c, 0)))[0]
        at = 0
        for p, lo, hi in [piece for member in members for piece in CHUNKS[member]]:
            size = cut(hi) - cut(lo)
            pieces[p].append((lo, rows[at : at + size]))
            at += size
    returned = {}
    for p in range(4):
        rows = [v for _, v in sorted(pieces[p], key=lambda piece: piece[0])]
        rows = rows[0] if len(rows) == 1 else jnp.concatenate(rows)
        rows = rows.reshape(per_part, slot_cap, feat_width)
        for q, j in enumerate(parts[p]):
            returned[j] = rows[q] if j == 0 else swap(rows[q], j)
    back = jnp.concatenate([returned[j] for j in range(n_groups)], axis=0)
    routed = dot32(pick, back, 0, 0)
    return (
        routed.astype(jnp.bfloat16),
        gate_up_grad,
        down_grad,
    )


def solution(mesh):
    placed = (
        P(("parts", "group", "local"), None),
        P(("parts", "group", "local"), None),
        P(("parts", "group", "local"), None),
        P(("parts", "group", "local"), None),
        P(("parts", "group", "local"), None),
        P("group", None, None, "local"),
        P("group", "local", None),
    )
    return jax.shard_map(
        per_device,
        mesh=mesh,
        in_specs=placed,
        out_specs=(
            P(("parts", "group", "local"), None),
            P(("parts", "group"), None, None, "local"),
            P(("parts", "group"), "local", None),
        ),
        check_vma=False,
    )
```
